32 devices in a mesh: box: 8 (over y, x, core), dir: 4 (over z).
Axes of the slice: x: 2, y: 2, z: 4, core: 2. Of those that a mesh axis runs over, the one named last changes fastest.
Arguments:
- child_field: float32 [2, 4, 256, 4608], P(None, None, 'box', 'dir'), may hold values from -6 to 6
- child_of: int32 [64, 4], P('box'), may hold values from 0 to 255, as said below
- shift_angle: float32 [4, 18432], P(None, 'dir'), may hold values from -3.140625 to 3.140625
- interp_index: int32 [6, 18432], P(None, 'dir'), may hold values from 0 to 4607, as said below
- interp_weight: float32 [6, 18432], P(None, 'dir'), may hold values from -0.2 to 0.5
- interaction_list: int32 [27, 64], replicated, may hold values from 0 to 63
- translation: float32 [2, 27, 18432], P(None, None, 'dir'), may hold values from -0.875 to 0.875
Outputs:
- child_incoming: float32 [2, 4, 256, 4608], P(None, None, 'box', 'dir')
The draws below stay inside these ranges and needn't reach their ends.
Inputs may be any that keep to these rules, and one draw needn't show every extreme that they name: child_of lists every child box once; the parents p with p // 8 = q have exactly the children q * 32 to (q + 1) * 32 - 1. interp_index[j, k] differs from k // 4 by at most 8, and for j = 0 by exactly 8 where k // 4 lies 8 or more from both ends.
All inputs are finite; a program needn't handle non-finite values.
Results may differ from the reference program's by a relative error of at most 0.00007.
Values sent between devices are 32-bit elements; how exact they have to be, the bound alone decides.
A program may use at most 64 MiB of HBM per device.

```python
import math
import jax
import jax.numpy as jnp
from jax import lax

K1 = 4608
K2 = 18432
RHS = 4
KIDS = 4
LIST = 27
STENCIL = 6
HW = 8
BOX_DEV = 32
NB = 256
NP = 64


def draw_child_of(key, part):
    group_count = NB // BOX_DEV
    keys = jax.random.split(jax.random.fold_in(key, 11), group_count)
    orders = jax.vmap(lambda single: jax.random.permutation(single, BOX_DEV))(keys)
    orders = orders + jnp.arange(group_count, dtype=jnp.int32)[:, None] * BOX_DEV
    return orders.reshape(NP, KIDS).astype(jnp.int32)


def draw_interp_index(key, part):
    offsets = jax.random.randint(jax.random.fold_in(key, 23), (STENCIL, K2), -HW, HW + 1)
    centres = jnp.arange(K2, dtype=jnp.int32)
    edges = jnp.where(centres % 2 == 0, -HW, HW).astype(jnp.int32)
    offsets = offsets.at[0].set(edges)
    return jnp.clip(centres // 4 + offsets, 0, K1 - 1).astype(jnp.int32)


def plant(drawn, rng, low, top_value):
    shape = drawn.shape
    place = [jax.random.randint(jax.random.fold_in(rng, axis), (), 0, shape[axis]) for axis in range(len(shape))]
    drawn = drawn.at[tuple(place)].set(low)
    longest = shape.index(max(shape))
    place[longest] = (place[longest] + 1) % shape[longest]
    return drawn.at[tuple(place)].set(top_value)


def level_of(key, extent, cuts, smallest, largest):
    factor_of = 1.0
    for axis_at, parts in cuts:
        draws = jax.random.uniform(jax.random.fold_in(jax.random.fold_in(key, 6), axis_at), (parts,), jnp.float32, smallest / len(cuts), largest / len(cuts))
        factor_of = factor_of * jnp.repeat(jnp.exp(draws), extent[axis_at] // parts).reshape((-1,) + (1,) * (len(extent) - 1 - axis_at))
    return factor_of


def bell_draw(own_key, extent, scale, reach, shards=(), kind=jnp.bfloat16):
    drawn = jax.random.normal(own_key, extent, jnp.float32) * scale
    if len(shards) > 0:
        drawn = level_of(own_key, extent, shards, -0.22, 0.18) * drawn
    return jnp.clip(drawn, min=-reach, max=reach).astype(kind)


def setup_inputs(seed: int = 0) -> dict:
    splits = jax.random.split(jax.random.key(seed), 8)
    return {
        "child_field": bell_draw(splits[0], (2, RHS, NB, K1), 1.0, 6.0, ((2, 8), (3, 4)), jnp.float32),
        "child_of": draw_child_of(jax.random.fold_in(splits[7], 71), 0),
        "shift_angle": jnp.clip(jax.random.uniform(splits[2], (KIDS, K2), jnp.float32, -3.140625, 3.140625), -3.140625, 3.140625),
        "interp_index": draw_interp_index(jax.random.fold_in(splits[7], 71), 0),
        "interp_weight": jnp.clip(-0.2 + 0.7 * jax.random.uniform(splits[4], (STENCIL, K2), jnp.float32) ** level_of(splits[4], (STENCIL, K2), ((1, 4),), -0.2, 0.2), -0.2, 0.5),
        "interaction_list": plant(jax.random.randint(splits[5], (LIST, NP), 0, NP), jax.random.fold_in(splits[5], 1), 0, NP - 1).astype(jnp.int32),
        "translation": bell_draw(splits[6], (2, LIST, K2), (2 * LIST) ** -0.5, 0.875, ((2, 4),), jnp.float32),
    }


def interpolate(values, index_table, weight_table):
    summed = jnp.zeros(values.shape[:-1] + (index_table.shape[1],), jnp.float32)
    for column in range(index_table.shape[0]):
        summed = summed + weight_table[column] * jnp.take(values, index_table[column], axis=-1)
    return summed


def anterpolate(values, index_table, weight_table):
    summed = jnp.zeros(values.shape[:-1] + (K1,), jnp.float32)
    for column in range(index_table.shape[0]):
        summed = summed.at[..., index_table[column]].add(weight_table[column] * values)
    return summed


def reference(child_field, child_of, shift_angle, interp_index, interp_weight, interaction_list, translation):
    cosines = jnp.cos(shift_angle)
    sine_part = jnp.sin(shift_angle)
    group_size = math.gcd(NP, 32)
    group_count = NP // group_size
    child_groups = child_of.reshape(group_count, group_size, KIDS)

    def aggregate(children):
        picked = child_field[:, :, children]
        spread = interpolate(picked, interp_index, interp_weight)
        real_part = jnp.sum(spread[0] * cosines - spread[1] * sine_part, axis=2)
        imag_part = jnp.sum(spread[0] * sine_part + spread[1] * cosines, axis=2)
        return jnp.stack([real_part, imag_part])

    outgoing = lax.map(aggregate, child_groups)
    outgoing = jnp.moveaxis(outgoing, 0, 2).reshape(2, RHS, NP, K2)

    def add_term(term, carry):
        source = jnp.take(outgoing, interaction_list[term], axis=2)
        op_real = translation[0, term]
        op_imag = translation[1, term]
        return jnp.stack([carry[0] + op_real * source[0] - op_imag * source[1],
                          carry[1] + op_real * source[1] + op_imag * source[0]])

    translated = lax.fori_loop(0, LIST, add_term, jnp.zeros_like(outgoing))

    def disaggregate(inputs):
        children, incoming = inputs
        real_part = incoming[0][:, :, None] * cosines + incoming[1][:, :, None] * sine_part
        imag_part = incoming[1][:, :, None] * cosines - incoming[0][:, :, None] * sine_part
        return anterpolate(jnp.stack([real_part, imag_part]), interp_index, interp_weight)

    grouped = jnp.moveaxis(translated.reshape(2, RHS, group_count, group_size, K2), 2, 0)
    pieces = lax.map(disaggregate, (child_groups, grouped))
    slots = jnp.moveaxis(pieces, 0, 2).reshape(2, RHS, NP * KIDS, K1)
    return jnp.zeros_like(child_field).at[:, :, child_of.reshape(-1)].set(slots)
```

```python
import jax
import jax.numpy as jnp
from jax import lax
from jax.experimental import pallas as pl
from jax.experimental.pallas import tpu as pltpu
from jax.sharding import PartitionSpec as P

HW = 8
LANES = 128
RATIO = 4
BAND = LANES // RATIO + 2 * HW
WINDOW = 2 * LANES
VMEM = pl.BlockSpec(memory_space=pltpu.VMEM)
SMEM = pl.BlockSpec(memory_space=pltpu.SMEM)


def rotated(value):
    half = value.shape[0] // 2
    sign = jnp.where(lax.broadcasted_iota(jnp.int32, value.shape, 0) < half, -1.0, 1.0)
    return pltpu.roll(value, half, 0) * sign


def split(value):
    high = value.astype(jnp.bfloat16)
    low = (value - high.astype(jnp.float32)).astype(jnp.bfloat16)
    return high, low


def lanes_of(chunk):
    return pl.ds(pl.multiple_of(chunk * LANES, LANES), LANES)


def band_of(chunk, first_child, index_ref, weight_ref):
    place = lax.broadcasted_iota(jnp.int32, (BAND, LANES), 0)
    base = first_child + chunk * (LANES // RATIO) - HW
    band = jnp.zeros((BAND, LANES), jnp.float32)
    for stencil_at in range(index_ref.shape[0]):
        row = index_ref[stencil_at : stencil_at + 1, lanes_of(chunk)] - base
        weight = weight_ref[stencil_at : stencil_at + 1, lanes_of(chunk)]
        band = band + jnp.where(row == place, weight, 0.0)
    return band


def band_rows(corner):
    return pl.ds(pl.multiple_of(corner * (LANES // RATIO), LANES // RATIO), BAND)


def aggregate_kernel(x_ref, cos_ref, sin_ref, index_ref, weight_ref, kids_ref, out_ref,
                     high_ref, low_ref, matrix_ref, field_ref):
    first_child = lax.axis_index("dir") * (index_ref.shape[1] // RATIO)
    high, low = split(x_ref[...])
    high_ref[...] = high
    low_ref[...] = low
    matrix_ref[...] = jnp.zeros_like(matrix_ref)
    parents, kids = kids_ref.shape

    def one(chunk, carry):
        corner = lax.rem(chunk, RATIO)
        columns = pl.ds(pl.multiple_of(chunk // RATIO * LANES, LANES), WINDOW)
        band_high, band_low = split(band_of(chunk, first_child, index_ref, weight_ref))
        matrix_ref[corner, band_rows(corner), :LANES] = band_high
        matrix_ref[corner, band_rows(corner), LANES:] = band_low
        both = jnp.dot(high_ref[:, columns], matrix_ref[corner],
                       preferred_element_type=jnp.float32)
        rest = jnp.dot(low_ref[:, columns], matrix_ref[corner, :, :LANES],
                       preferred_element_type=jnp.float32)
        field_ref[...] = (both[:, :LANES] + (both[:, LANES:] + rest)).reshape(field_ref.shape)
        cosines = cos_ref[:, lanes_of(chunk)]
        sines = sin_ref[:, lanes_of(chunk)]
        for parent in range(parents):
            straight = turned = 0.0
            for kid in range(kids):
                value = field_ref[kids_ref[parent, kid]]
                straight = straight + cosines[kid : kid + 1] * value
                turned = turned + sines[kid : kid + 1] * value
            out_ref[chunk, parent] = straight + rotated(turned)
        return carry

    lax.fori_loop(0, index_ref.shape[1] // LANES, one, 0)


def spread_kernel(in_ref, cos_ref, sin_ref, index_ref, weight_ref, slot_ref, out_ref,
                  twice_ref, low_ref, values_ref, phase_ref):
    first_child = lax.axis_index("dir") * (index_ref.shape[1] // RATIO)
    twice_ref[...] = jnp.zeros_like(twice_ref)
    low_ref[...] = jnp.zeros_like(low_ref)
    out_ref[...] = jnp.zeros_like(out_ref)
    boxes = slot_ref.shape[0]
    kids = cos_ref.shape[0]
    rows = out_ref.shape[0] // boxes

    def one(chunk, carry):
        corner = lax.rem(chunk, RATIO)
        columns = pl.ds(pl.multiple_of(chunk // RATIO * LANES, LANES), WINDOW)
        band_high, band_low = split(band_of(chunk, first_child, index_ref, weight_ref))
        twice_ref[corner, band_rows(corner), :LANES] = band_high
        twice_ref[corner, band_rows(corner), LANES:] = band_high
        low_ref[corner, band_rows(corner), :] = band_low
        for kid in range(kids):
            for half, table_ref in enumerate((cos_ref, sin_ref)):
                phase_ref[half, kid] = jnp.broadcast_to(
                    table_ref[kid : kid + 1, lanes_of(chunk)], phase_ref.shape[2:])
        for box in range(boxes):
            slot = slot_ref[box]
            value = in_ref[chunk, slot // kids]
            kid = lax.rem(slot, kids)
            cosine, sine = phase_ref[0, kid], phase_ref[1, kid]
            values_ref[box * rows : (box + 1) * rows, :] = cosine * value - sine * rotated(value)
        high, low = split(values_ref[...])
        dims = (((1,), (1,)), ((), ()))
        product = lax.dot_general(jnp.concatenate([high, low], axis=1), twice_ref[corner], dims,
                                  preferred_element_type=jnp.float32)
        product = product + lax.dot_general(high, low_ref[corner], dims,
                                            preferred_element_type=jnp.float32)
        out_ref[:, columns] += product
        return carry

    lax.fori_loop(0, index_ref.shape[1] // LANES, one, 0)


def exchange_kernel(out_ref, list_ref, table_ref, back_ref, answer, operator,
                    sent, arrived, returned, home, near, *source):
    chunks, parents = out_ref.shape[:2]
    count = lax.axis_size("box")
    me = lax.axis_index("box")
    terms = list_ref.shape[0]
    rounds = len(source)

    def first(owner):
        return chunks * owner // count

    def held(owner):
        return first(owner + 1) - first(owner)

    def other(step):
        return lax.rem(me + step, count)

    def block(owner):
        return pl.ds(owner * parents, parents)

    barrier = pltpu.get_barrier_semaphore()

    def greet(step, carry):
        pl.semaphore_signal(barrier, inc=1, device_id={"box": other(step)},
                            device_id_type=pl.DeviceIdType.MESH)
        return carry

    lax.fori_loop(1, count, greet, 0)
    pl.semaphore_wait(barrier, count - 1)

    def outbound(owner, at):
        chunk = first(owner) + at
        return pltpu.make_async_remote_copy(
            src_ref=out_ref.at[chunk], dst_ref=source[at].at[block(me)],
            send_sem=sent.at[chunk], recv_sem=arrived.at[at, me],
            device_id={"box": owner}, device_id_type=pl.DeviceIdType.MESH)

    def inbound(owner, at):
        return pltpu.make_async_remote_copy(
            src_ref=out_ref.at[first(me) + at], dst_ref=source[at].at[block(owner)],
            send_sem=sent.at[first(me) + at], recv_sem=arrived.at[at, owner],
            device_id={"box": owner}, device_id_type=pl.DeviceIdType.MESH)

    def homebound(owner, at):
        return pltpu.make_async_remote_copy(
            src_ref=answer.at[at, block(owner)], dst_ref=back_ref.at[first(me) + at],
            send_sem=returned.at[at, owner], recv_sem=home.at[first(me) + at],
            device_id={"box": owner}, device_id_type=pl.DeviceIdType.MESH)

    def from_owner(owner, at):
        return pltpu.make_async_remote_copy(
            src_ref=answer.at[at, block(me)], dst_ref=back_ref.at[first(owner) + at],
            send_sem=returned.at[at, me], recv_sem=home.at[first(owner) + at],
            device_id={"box": owner}, device_id_type=pl.DeviceIdType.MESH)

    def own_out(at):
        return pltpu.make_async_copy(out_ref.at[first(me) + at], source[at].at[block(me)],
                                     near.at[at])

    def own_back(at):
        return pltpu.make_async_copy(answer.at[at, block(me)], back_ref.at[first(me) + at],
                                     near.at[at])

    def each(act):
        def step_of(step, carry):
            act(other(step))
            return carry

        lax.fori_loop(1, count, step_of, 0)

    for at in range(rounds):

        def send(owner):
            pl.when(at < held(owner))(lambda: outbound(owner, at).start())

        each(send)
        pl.when(at < held(me))(lambda: own_out(at).start())

    def translate_group(at, owner):
        unroll = 3 if terms % 3 == 0 else 1

        def some(term_at, carry):
            straight, turned = list(carry[0]), list(carry[1])
            for part in range(unroll):
                term = term_at * unroll + part
                op_real = operator[0, term]
                op_imag = operator[1, term]
                for parent in range(parents):
                    value = source[at][list_ref[term, owner * parents + parent]]
                    straight[parent] = straight[parent] + op_real * value
                    turned[parent] = turned[parent] + op_imag * value
            return tuple(straight), tuple(turned)

        zero = jnp.zeros(answer.shape[2:], jnp.float32)
        straight, turned = lax.fori_loop(
            0, terms // unroll, some, ((zero,) * parents, (zero,) * parents))
        for parent in range(parents):
            answer[at, owner * parents + parent] = straight[parent] + rotated(turned[parent])

    for at in range(rounds):

        @pl.when(at < held(me))
        def _():
            each(lambda owner: inbound(owner, at).wait_recv())
            own_out(at).wait()
            for half in range(2):
                for term in range(terms):
                    operator[half, term] = jnp.broadcast_to(
                        table_ref[half, term : term + 1, lanes_of(first(me) + at)],
                        operator.shape[2:])

            def reply(owner):
                translate_group(at, owner)
                homebound(owner, at).start()

            each(reply)
            translate_group(at, me)
            own_back(at).start()

    for at in range(rounds):

        def finish(owner):
            @pl.when(at < held(owner))
            def _():
                outbound(owner, at).wait_send()
                from_owner(owner, at).wait_recv()

        each(finish)

        @pl.when(at < held(me))
        def _():
            each(lambda owner: homebound(owner, at).wait_send())
            own_back(at).wait()


def shards(
    child_field, child_of, shift_angle, interp_index, interp_weight, interaction_list, translation
):
    box_count = lax.axis_size("box")
    box_index = lax.axis_index("box")
    dir_count = lax.axis_size("dir")
    halves, fields, own_boxes, strip_child = child_field.shape
    parents, kids = child_of.shape
    strip_par = interp_index.shape[1]
    chunks = strip_par // LANES
    parts = halves * fields
    rows = own_boxes * parts
    rounds = -(-chunks // box_count)
    width = strip_child + LANES
    f32, bf16 = jnp.float32, jnp.bfloat16
    limit = 48 * 1024 * 1024

    forward = [(i, i + 1) for i in range(dir_count - 1)]
    backward = [(i + 1, i) for i in range(dir_count - 1)]
    by_box = jnp.transpose(child_field, (2, 0, 1, 3)).reshape(rows, strip_child)
    low = lax.ppermute(by_box[:, strip_child - HW :], "dir", forward)
    high = lax.ppermute(by_box[:, :HW], "dir", backward)
    extended = jnp.concatenate(
        [low, by_box, high, jnp.zeros((rows, width - strip_child - 2 * HW), f32)], axis=1)
    cosines = jnp.cos(shift_angle)
    sines = jnp.sin(shift_angle)
    local = child_of - box_index * own_boxes
    slots = jnp.sum(
        jnp.where(local.reshape(-1)[:, None] == lax.iota(jnp.int32, own_boxes)[None, :],
                  lax.iota(jnp.int32, parents * kids)[:, None], 0), axis=0).astype(jnp.int32)

    outgoing = pl.pallas_call(
        aggregate_kernel,
        out_shape=jax.ShapeDtypeStruct((chunks, parents, parts, LANES), f32),
        in_specs=[VMEM] * 5 + [SMEM],
        out_specs=VMEM,
        scratch_shapes=[
            pltpu.VMEM((rows, width), bf16),
            pltpu.VMEM((rows, width), bf16),
            pltpu.VMEM((RATIO, WINDOW, 2 * LANES), bf16),
            pltpu.VMEM((own_boxes, parts, LANES), f32),
        ],
        compiler_params=pltpu.CompilerParams(vmem_limit_bytes=limit),
    )(extended, cosines, sines, interp_index, interp_weight, local)

    incoming = pl.pallas_call(
        exchange_kernel,
        out_shape=jax.ShapeDtypeStruct((chunks, parents, parts, LANES), f32),
        in_specs=[VMEM, SMEM, VMEM],
        out_specs=VMEM,
        scratch_shapes=[
            pltpu.VMEM((rounds, box_count * parents, parts, LANES), f32),
            pltpu.VMEM((2, interaction_list.shape[0], parts, LANES), f32),
            pltpu.SemaphoreType.DMA((chunks,)),
            pltpu.SemaphoreType.DMA((rounds, box_count)),
            pltpu.SemaphoreType.DMA((rounds, box_count)),
            pltpu.SemaphoreType.DMA((chunks,)),
            pltpu.SemaphoreType.DMA((rounds,)),
            *[pltpu.VMEM((box_count * parents, parts, LANES), f32)] * rounds,
        ],
        compiler_params=pltpu.CompilerParams(
            collective_id=0, has_side_effects=True, vmem_limit_bytes=limit),
    )(outgoing, interaction_list, translation)

    widened = pl.pallas_call(
        spread_kernel,
        out_shape=jax.ShapeDtypeStruct((rows, width), f32),
        in_specs=[VMEM] * 5 + [SMEM],
        out_specs=VMEM,
        scratch_shapes=[
            pltpu.VMEM((RATIO, WINDOW, 2 * LANES), bf16),
            pltpu.VMEM((RATIO, WINDOW, LANES), bf16),
            pltpu.VMEM((rows, LANES), f32),
            pltpu.VMEM((2, kids, parts, LANES), f32),
        ],
        compiler_params=pltpu.CompilerParams(vmem_limit_bytes=limit),
    )(incoming, cosines, sines, interp_index, interp_weight, slots)

    from_below = lax.ppermute(widened[:, strip_child + HW : strip_child + 2 * HW], "dir", forward)
    from_above = lax.ppermute(widened[:, :HW], "dir", backward)
    inner = widened[:, HW : HW + strip_child]
    inner = inner + jnp.pad(from_below, ((0, 0), (0, strip_child - HW)))
    inner = inner + jnp.pad(from_above, ((0, 0), (strip_child - HW, 0)))
    return jnp.transpose(inner.reshape(own_boxes, halves, fields, strip_child), (1, 2, 0, 3))


def solution(mesh):
    in_specs = (
        P(None, None, "box", "dir"),
        P("box", None),
        P(None, "dir"),
        P(None, "dir"),
        P(None, "dir"),
        P(),
        P(None, None, "dir"),
    )
    out_specs = P(None, None, "box", "dir")
    return jax.shard_map(shards, mesh=mesh, in_specs=in_specs, out_specs=out_specs, check_vma=False)
```

```python
import jax
import jax.numpy as jnp
from jax import lax
from jax.experimental import pallas as pl
from jax.experimental.pallas import tpu as pltpu
from jax.sharding import PartitionSpec as P

HW = 8
LANES = 128
RATIO = 4
BAND = LANES // RATIO + 2 * HW
WINDOW = 2 * LANES
VMEM = pl.BlockSpec(memory_space=pltpu.VMEM)
SMEM = pl.BlockSpec(memory_space=pltpu.SMEM)


def rotated(value):
    half = value.shape[0] // 2
    sign = jnp.where(lax.broadcasted_iota(jnp.int32, value.shape, 0) < half, -1.0, 1.0)
    return pltpu.roll(value, half, 0) * sign


def split(value):
    high = value.astype(jnp.bfloat16)
    low = (value - high.astype(jnp.float32)).astype(jnp.bfloat16)
    return high, low


def lanes_of(chunk):
    return pl.ds(pl.multiple_of(chunk * LANES, LANES), LANES)


def band_of(chunk, first_child, index_ref, weight_ref):
    place = lax.broadcasted_iota(jnp.int32, (BAND, LANES), 0)
    base = first_child + chunk * (LANES // RATIO) - HW
    band = jnp.zeros((BAND, LANES), jnp.float32)
    for stencil_at in range(index_ref.shape[0]):
        row = index_ref[stencil_at : stencil_at + 1, lanes_of(chunk)] - base
        weight = weight_ref[stencil_at : stencil_at + 1, lanes_of(chunk)]
        band = band + jnp.where(row == place, weight, 0.0)
    return band


def band_rows(corner):
    return pl.ds(pl.multiple_of(corner * (LANES // RATIO), LANES // RATIO), BAND)


def whole_kernel(
    x_ref, cos_ref, sin_ref, index_ref, weight_ref, table_ref, kids_ref, parent_ref, kid_ref,
    list_ref, result_ref,
    high_ref, low_ref, bands, matrix_ref, field_ref, outgoing, answer, operator, back, piece, phase,
    values_ref, wide_ref, edge_in, edge_out, edge_back,
    sent, arrived, returned, home, near, edge_sent, edge_arrived, *source
):
    chunks, parents = outgoing.shape[:2]
    strip = x_ref.shape[1]
    rows = x_ref.shape[0]
    boxes = parent_ref.shape[0]
    parts = rows // boxes
    kids = cos_ref.shape[0]
    terms = list_ref.shape[0]
    rounds = len(source)
    count = lax.axis_size("box")
    me = lax.axis_index("box")
    layers = lax.axis_size("dir")
    layer = lax.axis_index("dir")
    first_child = layer * strip
    mesh_id = pl.DeviceIdType.MESH
    has_below = layer > 0
    has_above = layer < layers - 1

    def first(owner):
        return chunks * owner // count

    def held(owner):
        return first(owner + 1) - first(owner)

    def chunk_of(owner, at):
        return first(owner) + jnp.where(owner < count // 2, held(owner) - 1 - at, at)

    def other(step):
        return lax.rem(me + step, count)

    def block(owner):
        return pl.ds(owner * parents, parents)

    def each(act, stop=count):
        def step_of(step, carry):
            act(other(step))
            return carry

        lax.fori_loop(1, stop, step_of, 0)

    barrier = pltpu.get_barrier_semaphore()
    each(lambda owner: pl.semaphore_signal(
        barrier, inc=1, device_id={"box": owner}, device_id_type=mesh_id))

    @pl.when(has_below)
    def _():
        pl.semaphore_signal(barrier, inc=1, device_id={"dir": layer - 1}, device_id_type=mesh_id)

    @pl.when(has_above)
    def _():
        pl.semaphore_signal(barrier, inc=1, device_id={"dir": layer + 1}, device_id_type=mesh_id)

    neighbours = jnp.where(has_below, 1, 0) + jnp.where(has_above, 1, 0)
    pl.semaphore_wait(barrier, count - 1 + neighbours)

    def to_above(at, src, dst):
        return pltpu.make_async_remote_copy(
            src_ref=src, dst_ref=dst.at[0], send_sem=edge_sent.at[at, 0],
            recv_sem=edge_arrived.at[at, 0], device_id={"dir": layer + 1}, device_id_type=mesh_id)

    def to_below(at, src, dst):
        return pltpu.make_async_remote_copy(
            src_ref=src, dst_ref=dst.at[1], send_sem=edge_sent.at[at, 1],
            recv_sem=edge_arrived.at[at, 1], device_id={"dir": layer - 1}, device_id_type=mesh_id)

    top = x_ref.at[:, strip - LANES :]
    bottom = x_ref.at[:, :LANES]
    pl.when(has_above)(lambda: to_above(0, top, edge_in).start())
    pl.when(has_below)(lambda: to_below(0, bottom, edge_in).start())

    def outbound(owner, at):
        chunk = chunk_of(owner, at)
        return pltpu.make_async_remote_copy(
            src_ref=outgoing.at[chunk], dst_ref=source[at].at[block(me)],
            send_sem=sent.at[chunk], recv_sem=arrived.at[at, me],
            device_id={"box": owner}, device_id_type=mesh_id)

    def inbound(owner, at):
        chunk = chunk_of(me, at)
        return pltpu.make_async_remote_copy(
            src_ref=outgoing.at[chunk], dst_ref=source[at].at[block(owner)],
            send_sem=sent.at[chunk], recv_sem=arrived.at[at, owner],
            device_id={"box": owner}, device_id_type=mesh_id)

    def homebound(owner, at):
        chunk = chunk_of(me, at)
        return pltpu.make_async_remote_copy(
            src_ref=answer.at[at, block(owner)], dst_ref=back.at[chunk],
            send_sem=returned.at[at, owner], recv_sem=home.at[chunk],
            device_id={"box": owner}, device_id_type=mesh_id)

    def from_owner(owner, at):
        chunk = chunk_of(owner, at)
        return pltpu.make_async_remote_copy(
            src_ref=answer.at[at, block(me)], dst_ref=back.at[chunk],
            send_sem=returned.at[at, me], recv_sem=home.at[chunk],
            device_id={"box": owner}, device_id_type=mesh_id)

    def own_out(at):
        return pltpu.make_async_copy(outgoing.at[chunk_of(me, at)], source[at].at[block(me)],
                                     near.at[at])

    def own_back(at):
        return pltpu.make_async_copy(answer.at[at, block(me)], back.at[chunk_of(me, at)],
                                     near.at[at])

    extended = jnp.concatenate([x_ref[...], jnp.zeros((rows, LANES), jnp.float32)], axis=1)
    high, low = split(pltpu.roll(extended, HW, 1))
    high_ref[...] = high
    low_ref[...] = low
    matrix_ref[...] = jnp.zeros_like(matrix_ref)
    wide_ref[...] = jnp.zeros_like(wide_ref)
    lane = lax.broadcasted_iota(jnp.int32, (rows, LANES), 1)

    def put_edge(side, columns, begin):
        new_high, new_low = split(pltpu.roll(edge_in[side], HW, 1))
        chosen = ((lane >= begin) & (lane < begin + HW)).astype(jnp.bfloat16)
        keep = 1 - chosen
        high_ref[:, columns] = high_ref[:, columns] * keep + new_high * chosen
        low_ref[:, columns] = low_ref[:, columns] * keep + new_low * chosen

    def window_of(chunk):
        return pl.ds(pl.multiple_of(chunk // RATIO * LANES, LANES), WINDOW)

    def aggregate(chunk):
        corner = lax.rem(chunk, RATIO)
        columns = window_of(chunk)
        band_high, band_low = split(band_of(chunk, first_child, index_ref, weight_ref))
        bands[chunk, :, :LANES] = band_high
        bands[chunk, :, LANES:] = band_low
        matrix_ref[corner, band_rows(corner), :LANES] = band_high
        matrix_ref[corner, band_rows(corner), LANES:] = band_low
        both = jnp.dot(high_ref[:, columns], matrix_ref[corner],
                       preferred_element_type=jnp.float32)
        rest = jnp.dot(low_ref[:, columns], matrix_ref[corner, :, :LANES],
                       preferred_element_type=jnp.float32)
        field_ref[...] = (both[:, :LANES] + (both[:, LANES:] + rest)).reshape(field_ref.shape)
        cosines = cos_ref[:, lanes_of(chunk)]
        sines = sin_ref[:, lanes_of(chunk)]
        for parent in range(parents):
            straight = turned = 0.0
            for kid in range(kids):
                value = field_ref[kids_ref[parent, kid]]
                straight = straight + cosines[kid : kid + 1] * value
                turned = turned + sines[kid : kid + 1] * value
            outgoing[chunk, parent] = straight + rotated(turned)

    for at in range(rounds):
        if at == max(0, rounds - 2):

            @pl.when(has_below)
            def _():
                to_above(0, top, edge_in).wait_recv()
                put_edge(0, pl.ds(0, LANES), 0)

            @pl.when(has_above)
            def _():
                to_below(0, bottom, edge_in).wait_recv()
                put_edge(1, pl.ds(strip, LANES), HW)

        def produce(owner):
            @pl.when(at < held(owner))
            def _():
                aggregate(chunk_of(owner, at))
                pl.when(owner != me)(lambda: outbound(owner, at).start())
                pl.when(owner == me)(lambda: own_out(at).start())

        each(produce, count + 1)

    def translate_group(at, owner):
        unroll = 3 if terms % 3 == 0 else 1

        def some(term_at, carry):
            straight, turned = list(carry[0]), list(carry[1])
            for part in range(unroll):
                term = term_at * unroll + part
                op_real = operator[0, term]
                op_imag = operator[1, term]
                for parent in range(parents):
                    value = source[at][list_ref[term, owner * parents + parent]]
                    straight[parent] = straight[parent] + op_real * value
                    turned[parent] = turned[parent] + op_imag * value
            return tuple(straight), tuple(turned)

        zero = jnp.zeros(answer.shape[2:], jnp.float32)
        straight, turned = lax.fori_loop(
            0, terms // unroll, some, ((zero,) * parents, (zero,) * parents))
        for parent in range(parents):
            answer[at, owner * parents + parent] = straight[parent] + rotated(turned[parent])

    for at in range(rounds):

        @pl.when(at < held(me))
        def _():
            each(lambda owner: inbound(owner, at).wait_recv())
            own_out(at).wait()
            for half in range(2):
                for term in range(terms):
                    operator[half, term] = jnp.broadcast_to(
                        table_ref[half, term : term + 1, lanes_of(chunk_of(me, at))],
                        operator.shape[2:])

            def reply(owner):
                translate_group(at, owner)
                pl.when(owner != me)(lambda: homebound(owner, at).start())
                pl.when(owner == me)(lambda: own_back(at).start())

            each(reply, count + 1)

    def spread(chunk):
        corner = lax.rem(chunk, RATIO)
        matrix_ref[corner, band_rows(corner), :] = bands[chunk]
        for parent in range(parents):
            value = back[chunk, parent]
            piece[0, parent] = value
            piece[1, parent] = rotated(value)
        for kid in range(kids):
            for half, angles in enumerate((cos_ref, sin_ref)):
                phase[half, kid] = jnp.broadcast_to(
                    angles[kid : kid + 1, lanes_of(chunk)], phase.shape[2:])
        for box in range(boxes):
            parent, kid = parent_ref[box], kid_ref[box]
            values_ref[box * parts : (box + 1) * parts, :] = (
                phase[0, kid] * piece[0, parent] - phase[1, kid] * piece[1, parent])
        high, low = split(values_ref[...])
        dims = (((1,), (1,)), ((), ()))
        product = lax.dot_general(jnp.concatenate([high, high], axis=1), matrix_ref[corner], dims,
                                  preferred_element_type=jnp.float32)
        product = product + lax.dot_general(low, matrix_ref[corner, :, :LANES], dims,
                                            preferred_element_type=jnp.float32)
        wide_ref[:, window_of(chunk)] += product

    above_part = edge_out.at[0]
    below_part = edge_out.at[1]
    order = sorted(range(rounds), key=lambda at: (at > 0, at < rounds - 2, at))
    for place, at in enumerate(order):

        def finish(owner):
            @pl.when(at < held(owner))
            def _():
                @pl.when(owner != me)
                def _():
                    outbound(owner, at).wait_send()
                    from_owner(owner, at).wait_recv()

                pl.when(owner == me)(lambda: own_back(at).wait())
                spread(chunk_of(owner, at))

        each(finish, count + 1)

        @pl.when(at < held(me))
        def _():
            each(lambda owner: homebound(owner, at).wait_send())

        if place == min(2, rounds - 1):

            @pl.when(has_above)
            def _():
                edge_out[0] = wide_ref[:, strip:]
                to_above(1, above_part, edge_back).start()

            @pl.when(has_below)
            def _():
                edge_out[1] = wide_ref[:, :LANES]
                to_below(1, below_part, edge_back).start()

    @pl.when(has_below)
    def _():
        to_above(1, above_part, edge_back).wait_recv()
        mine = (lane >= HW) & (lane < 2 * HW)
        wide_ref[:, :LANES] += jnp.where(mine, edge_back[0], 0.0)
        to_below(0, bottom, edge_in).wait_send()
        to_below(1, below_part, edge_back).wait_send()

    @pl.when(has_above)
    def _():
        to_below(1, below_part, edge_back).wait_recv()
        wide_ref[:, strip:] += jnp.where(lane < HW, edge_back[1], 0.0)
        to_above(0, top, edge_in).wait_send()
        to_above(1, above_part, edge_back).wait_send()

    result_ref[...] = pltpu.roll(wide_ref[...], strip + LANES - HW, 1)[:, :strip]


def shards(
    child_field, child_of, shift_angle, interp_index, interp_weight, interaction_list, translation
):
    box_count = lax.axis_size("box")
    box_index = lax.axis_index("box")
    halves, fields, own_boxes, strip_child = child_field.shape
    parents, kids = child_of.shape
    chunks = interp_index.shape[1] // LANES
    parts = halves * fields
    rows = own_boxes * parts
    rounds = -(-chunks // box_count)
    width = strip_child + LANES
    terms = interaction_list.shape[0]
    f32, bf16 = jnp.float32, jnp.bfloat16

    by_box = jnp.transpose(child_field, (2, 0, 1, 3)).reshape(rows, strip_child)
    local = child_of - box_index * own_boxes
    slots = jnp.sum(
        jnp.where(local.reshape(-1)[:, None] == lax.iota(jnp.int32, own_boxes)[None, :],
                  lax.iota(jnp.int32, parents * kids)[:, None], 0), axis=0).astype(jnp.int32)

    result = pl.pallas_call(
        whole_kernel,
        out_shape=jax.ShapeDtypeStruct((rows, strip_child), f32),
        in_specs=[VMEM] * 6 + [SMEM] * 4,
        out_specs=VMEM,
        scratch_shapes=[
            pltpu.VMEM((rows, width), bf16),
            pltpu.VMEM((rows, width), bf16),
            pltpu.VMEM((chunks, BAND, 2 * LANES), bf16),
            pltpu.VMEM((RATIO, WINDOW, 2 * LANES), bf16),
            pltpu.VMEM((own_boxes, parts, LANES), f32),
            pltpu.VMEM((chunks, parents, parts, LANES), f32),
            pltpu.VMEM((rounds, box_count * parents, parts, LANES), f32),
            pltpu.VMEM((2, terms, parts, LANES), f32),
            pltpu.VMEM((chunks, parents, parts, LANES), f32),
            pltpu.VMEM((2, parents, parts, LANES), f32),
            pltpu.VMEM((2, kids, parts, LANES), f32),
            pltpu.VMEM((rows, LANES), f32),
            pltpu.VMEM((rows, width), f32),
            pltpu.VMEM((2, rows, LANES), f32),
            pltpu.VMEM((2, rows, LANES), f32),
            pltpu.VMEM((2, rows, LANES), f32),
            pltpu.SemaphoreType.DMA((chunks,)),
            pltpu.SemaphoreType.DMA((rounds, box_count)),
            pltpu.SemaphoreType.DMA((rounds, box_count)),
            pltpu.SemaphoreType.DMA((chunks,)),
            pltpu.SemaphoreType.DMA((rounds,)),
            pltpu.SemaphoreType.DMA((2, 2)),
            pltpu.SemaphoreType.DMA((2, 2)),
            *[pltpu.VMEM((box_count * parents, parts, LANES), f32)] * rounds,
        ],
        compiler_params=pltpu.CompilerParams(
            collective_id=0, has_side_effects=True, vmem_limit_bytes=48 * 1024 * 1024),
    )(by_box, jnp.cos(shift_angle), jnp.sin(shift_angle), interp_index, interp_weight, translation,
      local, slots // kids, slots % kids, interaction_list)
    return jnp.transpose(result.reshape(own_boxes, halves, fields, strip_child), (1, 2, 0, 3))


def solution(mesh):
    in_specs = (
        P(None, None, "box", "dir"),
        P("box", None),
        P(None, "dir"),
        P(None, "dir"),
        P(None, "dir"),
        P(),
        P(None, None, "dir"),
    )
    out_specs = P(None, None, "box", "dir")
    return jax.shard_map(shards, mesh=mesh, in_specs=in_specs, out_specs=out_specs, check_vma=False)
```

```python
import jax
import jax.numpy as jnp
from jax import lax
from jax.experimental import pallas as pl
from jax.experimental.pallas import tpu as pltpu
from jax.sharding import PartitionSpec as P

HW = 8
LANES = 128
RATIO = 4
BAND = LANES // RATIO + 2 * HW
WINDOW = 2 * LANES
VMEM = pl.BlockSpec(memory_space=pltpu.VMEM)
SMEM = pl.BlockSpec(memory_space=pltpu.SMEM)


def rotated(value):
    half = value.shape[0] // 2
    sign = jnp.where(lax.broadcasted_iota(jnp.int32, value.shape, 0) < half, -1.0, 1.0)
    return pltpu.roll(value, half, 0) * sign


def split(value):
    high = value.astype(jnp.bfloat16)
    low = (value - high.astype(jnp.float32)).astype(jnp.bfloat16)
    return high, low


def lanes_of(chunk):
    return pl.ds(pl.multiple_of(chunk * LANES, LANES), LANES)


def band_of(chunk, first_child, index_ref, weight_ref):
    place = lax.broadcasted_iota(jnp.int32, (BAND, LANES), 0)
    base = first_child + chunk * (LANES // RATIO) - HW
    band = jnp.zeros((BAND, LANES), jnp.float32)
    for stencil_at in range(index_ref.shape[0]):
        row = index_ref[stencil_at : stencil_at + 1, lanes_of(chunk)] - base
        weight = weight_ref[stencil_at : stencil_at + 1, lanes_of(chunk)]
        band = band + jnp.where(row == place, weight, 0.0)
    return band


def band_rows(corner):
    return pl.ds(pl.multiple_of(corner * (LANES // RATIO), LANES // RATIO), BAND)


def whole_kernel(
    x_ref, cos_ref, sin_ref, index_ref, weight_ref, table_ref, kids_ref, parent_ref, kid_ref,
    list_ref, result_ref,
    high_ref, low_ref, bands, matrix_0, matrix_1, field_0, field_1, outgoing, answer, operator, back,
    piece_0, piece_1, phase_0, phase_1, values_0, values_1, wide_ref, edge_in, edge_out, edge_back,
    sent, arrived, returned, home, near, edge_sent, edge_arrived, *source
):
    chunks, parents = outgoing.shape[:2]
    strip = x_ref.shape[1]
    rows = x_ref.shape[0]
    boxes = parent_ref.shape[0]
    parts = rows // boxes
    kids = cos_ref.shape[0]
    terms = table_ref.shape[1]
    rounds = answer.shape[0]
    count = lax.axis_size("box")
    groups = [range(at, min(at + 2, rounds - 1)) for at in range(0, rounds - 1, 2)]
    groups.append(range(rounds - 1, rounds))
    slot_of = {at: (g, at - group[0]) for g, group in enumerate(groups) for at in group}
    sets = [(matrix_0, field_0, piece_0, phase_0, values_0),
            (matrix_1, field_1, piece_1, phase_1, values_1)]
    many = 2 if count % 2 == 0 else 1
    me = lax.axis_index("box")
    layers = lax.axis_size("dir")
    layer = lax.axis_index("dir")
    first_child = layer * strip
    mesh_id = pl.DeviceIdType.MESH
    has_below = layer > 0
    has_above = layer < layers - 1

    def first(owner):
        return chunks * owner // count

    def held(owner):
        return first(owner + 1) - first(owner)

    def chunk_of(owner, at):
        return first(owner) + jnp.where(owner < count // 2, held(owner) - 1 - at, at)

    def other(step):
        return lax.rem(me + step, count)

    def block(owner):
        return pl.ds(owner * parents, parents)

    def landing(at, owner):
        group, inner = slot_of[at]
        return source[group].at[block(owner), inner]

    def each_set(act):
        def steps_of(step, carry):
            act([other(step * many + 1 + k) for k in range(many)])
            return carry

        lax.fori_loop(0, count // many, steps_of, 0)

    def each(act, stop=count):
        def step_of(step, carry):
            act(other(step))
            return carry

        lax.fori_loop(1, stop, step_of, 0)

    barrier = pltpu.get_barrier_semaphore()
    each(lambda owner: pl.semaphore_signal(
        barrier, inc=1, device_id={"box": owner}, device_id_type=mesh_id))

    @pl.when(has_below)
    def _():
        pl.semaphore_signal(barrier, inc=1, device_id={"dir": layer - 1}, device_id_type=mesh_id)

    @pl.when(has_above)
    def _():
        pl.semaphore_signal(barrier, inc=1, device_id={"dir": layer + 1}, device_id_type=mesh_id)

    neighbours = jnp.where(has_below, 1, 0) + jnp.where(has_above, 1, 0)
    pl.semaphore_wait(barrier, count - 1 + neighbours)

    def to_above(at, src, dst):
        return pltpu.make_async_remote_copy(
            src_ref=src, dst_ref=dst.at[0], send_sem=edge_sent.at[at, 0],
            recv_sem=edge_arrived.at[at, 0], device_id={"dir": layer + 1}, device_id_type=mesh_id)

    def to_below(at, src, dst):
        return pltpu.make_async_remote_copy(
            src_ref=src, dst_ref=dst.at[1], send_sem=edge_sent.at[at, 1],
            recv_sem=edge_arrived.at[at, 1], device_id={"dir": layer - 1}, device_id_type=mesh_id)

    top = x_ref.at[:, strip - LANES :]
    bottom = x_ref.at[:, :LANES]
    pl.when(has_above)(lambda: to_above(0, top, edge_in).start())
    pl.when(has_below)(lambda: to_below(0, bottom, edge_in).start())

    def outbound(owner, at):
        chunk = chunk_of(owner, at)
        return pltpu.make_async_remote_copy(
            src_ref=outgoing.at[chunk], dst_ref=landing(at, me),
            send_sem=sent.at[chunk], recv_sem=arrived.at[at, me],
            device_id={"box": owner}, device_id_type=mesh_id)

    def inbound(owner, at):
        chunk = chunk_of(me, at)
        return pltpu.make_async_remote_copy(
            src_ref=outgoing.at[chunk], dst_ref=landing(at, owner),
            send_sem=sent.at[chunk], recv_sem=arrived.at[at, owner],
            device_id={"box": owner}, device_id_type=mesh_id)

    def homebound(owner, at):
        chunk = chunk_of(me, at)
        return pltpu.make_async_remote_copy(
            src_ref=answer.at[at, block(owner)], dst_ref=back.at[chunk],
            send_sem=returned.at[at, owner], recv_sem=home.at[chunk],
            device_id={"box": owner}, device_id_type=mesh_id)

    def from_owner(owner, at):
        chunk = chunk_of(owner, at)
        return pltpu.make_async_remote_copy(
            src_ref=answer.at[at, block(me)], dst_ref=back.at[chunk],
            send_sem=returned.at[at, me], recv_sem=home.at[chunk],
            device_id={"box": owner}, device_id_type=mesh_id)

    def own_out(at):
        return pltpu.make_async_copy(outgoing.at[chunk_of(me, at)], landing(at, me),
                                     near.at[at])

    def own_back(at):
        return pltpu.make_async_copy(answer.at[at, block(me)], back.at[chunk_of(me, at)],
                                     near.at[at])

    extended = jnp.concatenate([x_ref[...], jnp.zeros((rows, LANES), jnp.float32)], axis=1)
    high, low = split(pltpu.roll(extended, HW, 1))
    high_ref[...] = high
    low_ref[...] = low
    matrix_0[...] = jnp.zeros_like(matrix_0)
    matrix_1[...] = jnp.zeros_like(matrix_1)
    wide_ref[...] = jnp.zeros_like(wide_ref)
    lane = lax.broadcasted_iota(jnp.int32, (rows, LANES), 1)

    def put_edge(side, columns, begin):
        new_high, new_low = split(pltpu.roll(edge_in[side], HW, 1))
        chosen = ((lane >= begin) & (lane < begin + HW)).astype(jnp.bfloat16)
        keep = 1 - chosen
        high_ref[:, columns] = high_ref[:, columns] * keep + new_high * chosen
        low_ref[:, columns] = low_ref[:, columns] * keep + new_low * chosen

    def window_of(chunk):
        return pl.ds(pl.multiple_of(chunk // RATIO * LANES, LANES), WINDOW)

    def aggregate(chunk, scratch):
        matrix_ref, field_ref = scratch[:2]
        corner = lax.rem(chunk, RATIO)
        columns = window_of(chunk)
        band_high, band_low = split(band_of(chunk, first_child, index_ref, weight_ref))
        bands[chunk, :, :LANES] = band_high
        bands[chunk, :, LANES:] = band_low
        matrix_ref[corner, band_rows(corner), :LANES] = band_high
        matrix_ref[corner, band_rows(corner), LANES:] = band_low
        both = jnp.dot(high_ref[:, columns], matrix_ref[corner],
                       preferred_element_type=jnp.float32)
        rest = jnp.dot(low_ref[:, columns], matrix_ref[corner, :, :LANES],
                       preferred_element_type=jnp.float32)
        field_ref[...] = (both[:, :LANES] + (both[:, LANES:] + rest)).reshape(field_ref.shape)
        cosines = cos_ref[:, lanes_of(chunk)]
        sines = sin_ref[:, lanes_of(chunk)]
        for parent in range(parents):
            straight = turned = 0.0
            for kid in range(kids):
                value = field_ref[kids_ref[parent, kid]]
                straight = straight + cosines[kid : kid + 1] * value
                turned = turned + sines[kid : kid + 1] * value
            outgoing[chunk, parent] = straight + rotated(turned)

    for at in range(rounds):
        if at == max(0, rounds - 2):

            @pl.when(has_below)
            def _():
                to_above(0, top, edge_in).wait_recv()
                put_edge(0, pl.ds(0, LANES), 0)

            @pl.when(has_above)
            def _():
                to_below(0, bottom, edge_in).wait_recv()
                put_edge(1, pl.ds(strip, LANES), HW)

        def ship(owner):
            pl.when(owner != me)(lambda: outbound(owner, at).start())
            pl.when(owner == me)(lambda: own_out(at).start())

        def produce(owner):
            @pl.when(at < held(owner))
            def _():
                aggregate(chunk_of(owner, at), sets[0])
                ship(owner)

        def produce_set(owners):
            for owner, scratch in zip(owners, sets):
                aggregate(chunk_of(owner, at), scratch)
            for owner in owners:
                ship(owner)

        if at < rounds - 1:
            each_set(produce_set)
        else:
            each(produce, count + 1)

    def translate_group(group, owner):
        landed = source[group]
        inner = range(len(groups[group]))
        straight = {}
        turned = {}
        for term in range(terms):
            op_real = [operator[at, 0, term] for at in inner]
            op_imag = [operator[at, 1, term] for at in inner]
            for parent in range(parents):
                index = list_ref[(owner * terms + term) * parents + parent]
                for at in inner:
                    value = landed[index, at]
                    real, imag = op_real[at] * value, op_imag[at] * value
                    key = (parent, at)
                    straight[key] = straight[key] + real if term else real
                    turned[key] = turned[key] + imag if term else imag
        for parent, at in straight:
            answer[groups[group][at], owner * parents + parent] = (
                straight[parent, at] + rotated(turned[parent, at]))

    for group, members in enumerate(groups):

        def serve():
            for inner, at in enumerate(members):
                each(lambda owner: inbound(owner, at).wait_recv())
                own_out(at).wait()
                for half in range(2):
                    for term in range(terms):
                        operator[inner, half, term] = jnp.broadcast_to(
                            table_ref[half, term : term + 1, lanes_of(chunk_of(me, at))],
                            operator.shape[3:])

            def reply(owner):
                translate_group(group, owner)
                for at in members:
                    pl.when(owner != me)(lambda: homebound(owner, at).start())
                    pl.when(owner == me)(lambda: own_back(at).start())

            each(reply, count + 1)

        pl.when(members[0] < held(me))(serve)

    def spread(chunk, scratch):
        matrix_ref, _, piece, phase, values_ref = scratch
        corner = lax.rem(chunk, RATIO)
        matrix_ref[corner, band_rows(corner), :] = bands[chunk]
        for parent in range(parents):
            value = back[chunk, parent]
            piece[0, parent] = value
            piece[1, parent] = rotated(value)
        for kid in range(kids):
            for half, angles in enumerate((cos_ref, sin_ref)):
                phase[half, kid] = jnp.broadcast_to(
                    angles[kid : kid + 1, lanes_of(chunk)], phase.shape[2:])
        for box in range(boxes):
            parent, kid = parent_ref[box], kid_ref[box]
            values_ref[box * parts : (box + 1) * parts, :] = (
                phase[0, kid] * piece[0, parent] - phase[1, kid] * piece[1, parent])
        high, low = split(values_ref[...])
        dims = (((1,), (1,)), ((), ()))
        product = lax.dot_general(jnp.concatenate([high, high], axis=1), matrix_ref[corner], dims,
                                  preferred_element_type=jnp.float32)
        product = product + lax.dot_general(low, matrix_ref[corner, :, :LANES], dims,
                                            preferred_element_type=jnp.float32)
        return product

    above_part = edge_out.at[0]
    below_part = edge_out.at[1]
    order = sorted(range(rounds), key=lambda at: (at > 0, at < rounds - 2, at))
    for place, at in enumerate(order):

        def await_back(owner):
            @pl.when(owner != me)
            def _():
                outbound(owner, at).wait_send()
                from_owner(owner, at).wait_recv()

            pl.when(owner == me)(lambda: own_back(at).wait())

        def finish(owner):
            @pl.when(at < held(owner))
            def _():
                await_back(owner)
                chunk = chunk_of(owner, at)
                wide_ref[:, window_of(chunk)] += spread(chunk, sets[0])

        def finish_set(owners):
            for owner in owners:
                await_back(owner)
            at_chunks = [chunk_of(owner, at) for owner in owners]
            products = [spread(chunk, scratch) for chunk, scratch in zip(at_chunks, sets)]
            for chunk, product in zip(at_chunks, products):
                wide_ref[:, window_of(chunk)] += product

        if at < rounds - 1:
            each_set(finish_set)
        else:
            each(finish, count + 1)

        @pl.when(at < held(me))
        def _():
            each(lambda owner: homebound(owner, at).wait_send())

        if place == min(2, rounds - 1):

            @pl.when(has_above)
            def _():
                edge_out[0] = wide_ref[:, strip:]
                to_above(1, above_part, edge_back).start()

            @pl.when(has_below)
            def _():
                edge_out[1] = wide_ref[:, :LANES]
                to_below(1, below_part, edge_back).start()

    @pl.when(has_below)
    def _():
        to_above(1, above_part, edge_back).wait_recv()
        mine = (lane >= HW) & (lane < 2 * HW)
        wide_ref[:, :LANES] += jnp.where(mine, edge_back[0], 0.0)
        to_below(0, bottom, edge_in).wait_send()
        to_below(1, below_part, edge_back).wait_send()

    @pl.when(has_above)
    def _():
        to_below(1, below_part, edge_back).wait_recv()
        wide_ref[:, strip:] += jnp.where(lane < HW, edge_back[1], 0.0)
        to_above(0, top, edge_in).wait_send()
        to_above(1, above_part, edge_back).wait_send()

    result_ref[...] = pltpu.roll(wide_ref[...], strip + LANES - HW, 1)[:, :strip]


def shards(
    child_field, child_of, shift_angle, interp_index, interp_weight, interaction_list, translation
):
    box_count = lax.axis_size("box")
    box_index = lax.axis_index("box")
    halves, fields, own_boxes, strip_child = child_field.shape
    parents, kids = child_of.shape
    chunks = interp_index.shape[1] // LANES
    parts = halves * fields
    rows = own_boxes * parts
    rounds = -(-chunks // box_count)
    width = strip_child + LANES
    terms = interaction_list.shape[0]
    f32, bf16 = jnp.float32, jnp.bfloat16

    by_box = jnp.transpose(child_field, (2, 0, 1, 3)).reshape(rows, strip_child)
    local = child_of - box_index * own_boxes
    slots = jnp.sum(
        jnp.where(local.reshape(-1)[:, None] == lax.iota(jnp.int32, own_boxes)[None, :],
                  lax.iota(jnp.int32, parents * kids)[:, None], 0), axis=0).astype(jnp.int32)

    lists = jnp.transpose(interaction_list.reshape(terms, box_count, parents), (1, 0, 2))

    result = pl.pallas_call(
        whole_kernel,
        out_shape=jax.ShapeDtypeStruct((rows, strip_child), f32),
        in_specs=[VMEM] * 6 + [SMEM] * 4,
        out_specs=VMEM,
        scratch_shapes=[
            pltpu.VMEM((rows, width), bf16),
            pltpu.VMEM((rows, width), bf16),
            pltpu.VMEM((chunks, BAND, 2 * LANES), bf16),
            *[pltpu.VMEM((RATIO, WINDOW, 2 * LANES), bf16)] * 2,
            *[pltpu.VMEM((own_boxes, parts, LANES), f32)] * 2,
            pltpu.VMEM((chunks, parents, parts, LANES), f32),
            pltpu.VMEM((rounds, box_count * parents, parts, LANES), f32),
            pltpu.VMEM((2, 2, terms, parts, LANES), f32),
            pltpu.VMEM((chunks, parents, parts, LANES), f32),
            *[pltpu.VMEM((2, parents, parts, LANES), f32)] * 2,
            *[pltpu.VMEM((2, kids, parts, LANES), f32)] * 2,
            *[pltpu.VMEM((rows, LANES), f32)] * 2,
            pltpu.VMEM((rows, width), f32),
            pltpu.VMEM((2, rows, LANES), f32),
            pltpu.VMEM((2, rows, LANES), f32),
            pltpu.VMEM((2, rows, LANES), f32),
            pltpu.SemaphoreType.DMA((chunks,)),
            pltpu.SemaphoreType.DMA((rounds, box_count)),
            pltpu.SemaphoreType.DMA((rounds, box_count)),
            pltpu.SemaphoreType.DMA((chunks,)),
            pltpu.SemaphoreType.DMA((rounds,)),
            pltpu.SemaphoreType.DMA((2, 2)),
            pltpu.SemaphoreType.DMA((2, 2)),
            *[pltpu.VMEM((box_count * parents, min(2, rounds - 1 - at), parts, LANES), f32)
              for at in range(0, rounds - 1, 2)],
            pltpu.VMEM((box_count * parents, 1, parts, LANES), f32),
        ],
        compiler_params=pltpu.CompilerParams(
            collective_id=0, has_side_effects=True, vmem_limit_bytes=48 * 1024 * 1024),
    )(by_box, jnp.cos(shift_angle), jnp.sin(shift_angle), interp_index, interp_weight, translation,
      local, slots // kids, slots % kids, lists.reshape(-1))
    return jnp.transpose(result.reshape(own_boxes, halves, fields, strip_child), (1, 2, 0, 3))


def solution(mesh):
    in_specs = (
        P(None, None, "box", "dir"),
        P("box", None),
        P(None, "dir"),
        P(None, "dir"),
        P(None, "dir"),
        P(),
        P(None, None, "dir"),
    )
    out_specs = P(None, None, "box", "dir")
    return jax.shard_map(shards, mesh=mesh, in_specs=in_specs, out_specs=out_specs, check_vma=False)
```
